512 devices in a mesh: gx: 8 (over y), gy: 4 (over x), gz: 16 (over z, core).
Axes of the slice: x: 4, y: 8, z: 8, core: 2. Of those that a mesh axis runs over, the one named last changes fastest.
Arguments:
- patches: float32 [1024, 6, 16, 256], P(('gx', 'gy', 'gz')), may hold values from -2 to 6, as said below
- new_owner: int32 [1024], P(('gx', 'gy')), may hold values from 0 to 511, as said below
- new_slot: int32 [1024], P(('gx', 'gy')), may hold values from 0 to 3, as said below
Outputs:
- new_state: float32 [2048, 6, 16, 256], P(('gx', 'gy', 'gz'))
The draws below stay inside these ranges and needn't reach their ends.
Inputs may be any that keep to these rules, and one draw needn't show every extreme that they name: `patches`: each cell has density and pressure in [0.5, 2], velocity components in [-1, 1] and mass fraction in [0, 1]; momenta, energy and species density follow from these with the energy law of the steps. `new_owner`: A patch's new owner is its old owner p // 2 or the device whose index along gz differs from the old owner's in its lowest bit; within each group along gz the patches, in order of id, go to the group's devices in order of device index in contiguous runs; a device receives 0 to 4 patches, and in every group some device receives exactly 4. `new_slot`: the position of the patch in its new owner's run, so each device's used slots are 0 up to its count minus one.
All inputs are finite; a program needn't handle non-finite values.
Results may differ from the reference program's by a relative error of at most 0.0001.
Values sent between devices are 32-bit elements; how exact they have to be, the bound alone decides.
No kernel may reach another device: no remote copies, remote signals or barrier semaphores. Data moves between devices by JAX's collectives and lax.ppermute only.
A program may use at most 64 MiB of HBM per device.

```python
import jax
import jax.numpy as jnp
from jax import lax

EDGE = 16
GHOST = 4
FIELDS = 6
SLOT_DEV = 2
CAP = 4
PATCHES = 1024
N_GX = 8
N_GY = 4
N_GZ = 16


def regrid_plan(key):
    group_total = N_GX * N_GY
    members = N_GZ * SLOT_DEV
    half = N_GZ // 2

    def one_group(group):
        group_key = jax.random.fold_in(key, group)
        kinds = jax.random.randint(jax.random.fold_in(group_key, 1), (half,), 0, 5)
        table = jnp.array([0, 1, -1, SLOT_DEV, -SLOT_DEV], jnp.int32)
        delta = jnp.take(table, kinds)
        forced = jax.random.randint(jax.random.fold_in(group_key, 2), (), 0, half)
        sign = jax.random.randint(jax.random.fold_in(group_key, 3), (), 0, 2) * 2 - 1
        delta = jnp.where(jnp.arange(half, dtype=jnp.int32) == forced, SLOT_DEV * sign, delta)
        counts = jnp.stack([SLOT_DEV + delta, SLOT_DEV - delta], axis=1).reshape(N_GZ).astype(jnp.int32)
        ends = jnp.cumsum(counts)
        starts = ends - counts
        member = jnp.arange(members, dtype=jnp.int32)
        owner_local = jnp.sum((ends[None, :] <= member[:, None]).astype(jnp.int32), axis=1)
        slot = member - jnp.take(starts, owner_local)
        return ((group * N_GZ + owner_local).astype(jnp.int32), slot.astype(jnp.int32))
    owners, slots = jax.vmap(one_group)(jnp.arange(group_total, dtype=jnp.int32))
    return (owners.reshape(PATCHES), slots.reshape(PATCHES))


def draw_new_owner(key, part):
    owners, slots = regrid_plan(key)
    return owners


def draw_new_slot(key, part):
    owners, slots = regrid_plan(key)
    return slots


def draw_patches(key, part):
    key = jax.random.fold_in(key, 11)
    shape = (PATCHES, EDGE, EDGE * EDGE)
    keys = jax.random.split(key, 6)
    samples = [jax.random.uniform(keys[index], shape, jnp.float32) for index in range(6)]
    dens_level = samples[0]
    pres_level = samples[4]
    speeds = [2.0 * samples[index] - 1.0 for index in range(1, 4)]
    density = 0.5 * 4.0 ** dens_level
    pressure = 0.5 * 4.0 ** pres_level
    fraction = samples[5]
    kinetic = 0.5 * density * (speeds[0] * speeds[0] + speeds[1] * speeds[1] + speeds[2] * speeds[2])
    energy = pressure * 1.5 + kinetic
    fields = [density, density * speeds[0], density * speeds[1], density * speeds[2], energy, density * fraction]
    return jnp.stack(fields, axis=1).astype(jnp.float32)


def setup_inputs(seed: int = 0) -> dict:
    seeds = jax.random.split(jax.random.key(seed), 4)
    return {
        "patches": draw_patches(jax.random.fold_in(seeds[3], 71), 0),
        "new_owner": draw_new_owner(jax.random.fold_in(seeds[3], 71), 0),
        "new_slot": draw_new_slot(jax.random.fold_in(seeds[3], 71), 0),
    }


GAMMA = 5.0 / 3.0
STEP_RATIO = 0.08

def median_three(first, second, third):
    return jnp.maximum(jnp.minimum(first, second), jnp.minimum(jnp.maximum(first, second), third))

def to_primitive(conserved):
    density = conserved[0]
    velocity = conserved[1:4] / density
    pressure = (GAMMA - 1.0) * (conserved[4] - 0.5 * density * lax.optimization_barrier(jnp.sum(velocity * velocity, axis=0)))
    fraction = conserved[5] / density
    return jnp.concatenate([density[None], velocity, pressure[None], fraction[None]], axis=0)

def face_flux(primitive, normal):
    density = primitive[0]
    velocity = primitive[1:4]
    pressure = primitive[4]
    fraction = primitive[5]
    speed = velocity[normal]
    energy = pressure / (GAMMA - 1.0) + 0.5 * density * lax.optimization_barrier(jnp.sum(velocity * velocity, axis=0))
    conserved = jnp.concatenate([density[None], density * velocity, energy[None], (density * fraction)[None]], axis=0)
    flux = conserved * speed
    flux = flux.at[1 + normal].add(pressure)
    flux = flux.at[4].add(pressure * speed)
    signal = jnp.abs(speed) + jnp.sqrt(GAMMA * pressure / density)
    return (conserved, flux, signal)

def sweep(extended, normal):
    primitive = to_primitive(extended)
    length = primitive.shape[1]
    interior_count = length - 8
    left_cell = primitive[:, 2:length - 3]
    right_cell = primitive[:, 3:length - 2]
    face = (37.0 * (left_cell + right_cell) - 8.0 * (primitive[:, 1:length - 4] + primitive[:, 4:length - 1]) + (primitive[:, 0:length - 5] + primitive[:, 5:length])) / 60.0
    face = jnp.clip(face, jnp.minimum(left_cell, right_cell), jnp.maximum(left_cell, right_cell))
    centre = primitive[:, 3:length - 3]
    left_jump = centre - face[:, :-1]
    right_jump = face[:, 1:] - centre
    zeros = jnp.zeros_like(centre)
    right_limited = median_three(zeros, right_jump, 2.0 * left_jump)
    left_limited = median_three(zeros, left_jump, 2.0 * right_jump)
    plus_state = centre + right_limited
    minus_state = centre - left_limited
    left_state = plus_state[:, 0:interior_count + 1]
    right_state = minus_state[:, 1:interior_count + 2]
    left_cons, left_flux, left_signal = face_flux(left_state, normal)
    right_cons, right_flux, right_signal = face_flux(right_state, normal)
    signal = jnp.maximum(left_signal, right_signal)
    flux = 0.5 * (left_flux + right_flux) - 0.5 * signal * (right_cons - left_cons)
    return flux[:, 1:] - flux[:, :-1]

def advance_patch(package):
    fields_count = package.shape[0]
    plane = package.shape[2]
    side_cells = package.shape[2] // package.shape[2] * int(round_side(plane))
    depth = (package.shape[1] - side_cells) // 6
    interior = package[:, :side_cells]
    pieces = [package[:, side_cells + k * depth:side_cells + (k + 1) * depth] for k in range(6)]
    cube = interior.reshape(fields_count, side_cells, side_cells, side_cells)
    div_x = sweep(jnp.concatenate([pieces[0], interior, pieces[1]], axis=1), 0)
    y_major = cube.transpose(0, 2, 1, 3).reshape(fields_count, side_cells, plane)
    div_y = sweep(jnp.concatenate([pieces[2], y_major, pieces[3]], axis=1), 1)
    div_y = div_y.reshape(fields_count, side_cells, side_cells, side_cells).transpose(0, 2, 1, 3).reshape(fields_count, side_cells, plane)
    z_major = cube.transpose(0, 3, 1, 2).reshape(fields_count, side_cells, plane)
    div_z = sweep(jnp.concatenate([pieces[4], z_major, pieces[5]], axis=1), 2)
    div_z = div_z.reshape(fields_count, side_cells, side_cells, side_cells).transpose(0, 2, 3, 1).reshape(fields_count, side_cells, plane)
    return interior - STEP_RATIO * (div_x + div_y + div_z)

def round_side(plane):
    side = 1
    while side * side < plane:
        side = side + 1
    return side

def locate(pos_x, pos_y, pos_z):
    return (pos_x // SLOT_DEV * N_GY * N_GZ + pos_y * N_GZ + pos_z) * SLOT_DEV + pos_x % SLOT_DEV

def package_of(patches, patch_id):
    block = patch_id // SLOT_DEV
    pos_x = block // (N_GY * N_GZ) * SLOT_DEV + patch_id % SLOT_DEV
    pos_y = block // N_GZ % N_GY
    pos_z = block % N_GZ
    width_x = SLOT_DEV * N_GX
    plane = EDGE * EDGE
    lower_x = patches[locate((pos_x - 1) % width_x, pos_y, pos_z)][:, EDGE - GHOST:]
    upper_x = patches[locate((pos_x + 1) % width_x, pos_y, pos_z)][:, :GHOST]
    cube_low_y = patches[locate(pos_x, (pos_y - 1) % N_GY, pos_z)].reshape(FIELDS, EDGE, EDGE, EDGE)
    cube_high_y = patches[locate(pos_x, (pos_y + 1) % N_GY, pos_z)].reshape(FIELDS, EDGE, EDGE, EDGE)
    lower_y = cube_low_y[:, :, EDGE - GHOST:, :].transpose(0, 2, 1, 3).reshape(FIELDS, GHOST, plane)
    upper_y = cube_high_y[:, :, :GHOST, :].transpose(0, 2, 1, 3).reshape(FIELDS, GHOST, plane)
    cube_low_z = patches[locate(pos_x, pos_y, (pos_z - 1) % N_GZ)].reshape(FIELDS, EDGE, EDGE, EDGE)
    cube_high_z = patches[locate(pos_x, pos_y, (pos_z + 1) % N_GZ)].reshape(FIELDS, EDGE, EDGE, EDGE)
    lower_z = cube_low_z[:, :, :, EDGE - GHOST:].transpose(0, 3, 1, 2).reshape(FIELDS, GHOST, plane)
    upper_z = cube_high_z[:, :, :, :GHOST].transpose(0, 3, 1, 2).reshape(FIELDS, GHOST, plane)
    return jnp.concatenate([patches[patch_id], lower_x, upper_x, lower_y, upper_y, lower_z, upper_z], axis=1)

def reference(patches, new_owner, new_slot):
    initial = jnp.zeros((N_GX * N_GY * N_GZ * CAP, FIELDS, EDGE, EDGE * EDGE), patches.dtype)

    def place(patch_id, output):
        advanced = advance_patch(package_of(patches, patch_id))
        row = (new_owner[patch_id] * CAP + new_slot[patch_id]).astype(jnp.int32)
        zero = jnp.zeros((), jnp.int32)
        return lax.dynamic_update_slice(output, advanced[None].astype(output.dtype), (row, zero, zero, zero))
    return lax.fori_loop(0, PATCHES, place, initial)
```

```python
import functools

import jax
import jax.numpy as jnp
from jax import lax
from jax.experimental import pallas as pl
from jax.experimental.pallas import tpu as pltpu
from jax.sharding import PartitionSpec as P

EDGE = 16
GHOST = 4
CAP = 4
FIELDS = 6
PLANE = EDGE * EDGE
STRIP = GHOST * EDGE

STEP_RATIO = 0.08
VMEM = pl.BlockSpec(memory_space=pltpu.VMEM)
SMEM = pl.BlockSpec(memory_space=pltpu.SMEM)


def to_primitive(u):
    density, mom_x, mom_y, mom_z, energy, species = u
    inverse = 1.0 / density
    vel_x, vel_y, vel_z = mom_x * inverse, mom_y * inverse, mom_z * inverse
    kinetic = 0.5 * (mom_x * vel_x + mom_y * vel_y + mom_z * vel_z)
    pressure = (2.0 / 3.0) * (energy - kinetic)
    return [density, vel_x, vel_y, vel_z, pressure, species * inverse]


def median_zero(second, third):
    return jnp.maximum(jnp.minimum(second, 0.0), jnp.minimum(jnp.maximum(second, 0.0), third))


def side_terms(state, normal):
    density, pressure = state[0], state[4]
    ratio = pressure / density
    speed = state[1 + normal]
    square = state[1] * state[1] + state[2] * state[2] + state[3] * state[3]
    specific = 1.5 * ratio + 0.5 * square
    signal = jnp.abs(speed) + jnp.sqrt((5.0 / 3.0) * ratio)
    return speed, specific, signal


def sweep(primitive, normal, at):
    plus, minus = [], []
    for value in primitive:
        after = at(value, 1)
        face = 37.0 * (value + after) - 8.0 * (at(value, -1) + at(value, 2)) + (at(value, -2) + at(value, 3))
        face = face * (1.0 / 60.0)
        face = jnp.minimum(jnp.maximum(face, jnp.minimum(value, after)), jnp.maximum(value, after))
        left_jump = value - at(face, -1)
        right_jump = face - value
        plus.append(value + median_zero(right_jump, 2.0 * left_jump))
        minus.append(at(value - median_zero(left_jump, 2.0 * right_jump), 1))
    left_speed, left_specific, left_signal = side_terms(plus, normal)
    right_speed, right_specific, right_signal = side_terms(minus, normal)
    signal = jnp.maximum(left_signal, right_signal)
    left_weight = 0.5 * plus[0] * (left_speed + signal)
    right_weight = 0.5 * minus[0] * (right_speed - signal)
    flux = [left_weight + right_weight]
    for k in (1, 2, 3):
        flux.append(left_weight * plus[k] + right_weight * minus[k])
    flux[1 + normal] = flux[1 + normal] + 0.5 * (plus[4] + minus[4])
    flux.append(
        left_weight * left_specific
        + right_weight * right_specific
        + 0.5 * (plus[4] * left_speed + minus[4] * right_speed)
    )
    flux.append(left_weight * plus[5] + right_weight * minus[5])
    return [f - at(f, -1) for f in flux]


def exchange_lanes(rows):
    source = lax.broadcasted_iota(jnp.int32, (PLANE, PLANE), 0)
    target = lax.broadcasted_iota(jnp.int32, (PLANE, PLANE), 1)
    wanted = (target % EDGE) * EDGE + target // EDGE
    swap = jnp.where(source == wanted, 1.0, 0.0).astype(jnp.bfloat16)
    total = None
    for _ in range(3):
        part = rows.astype(jnp.bfloat16)
        moved = jnp.dot(part, swap, preferred_element_type=jnp.float32)
        total = moved if total is None else total + moved
        rows = rows - part.astype(jnp.float32)
    return total


def pack_kernel(u_ref, prim_ref, prim_z_ref, x_up, x_down, y_up, y_down, z_up, z_down):
    slots = u_ref.shape[0]
    for p in range(slots):
        for q, value in enumerate(to_primitive([u_ref[p, q] for q in range(FIELDS)])):
            prim_ref[p, q] = value
    flat = prim_ref[...].reshape(slots * FIELDS * EDGE, PLANE)
    prim_z_ref[...] = exchange_lanes(flat).reshape(slots, FIELDS, EDGE, PLANE)
    x_up[...] = prim_ref[slots - 1, :, EDGE - GHOST :, :]
    x_down[...] = prim_ref[0, :, :GHOST, :]
    for p in range(slots):
        lanes = slice(p * STRIP, (p + 1) * STRIP)
        y_up[:, :, lanes] = prim_ref[p, :, :, PLANE - STRIP :]
        y_down[:, :, lanes] = prim_ref[p, :, :, :STRIP]
        z_up[:, :, lanes] = prim_z_ref[p, :, :, PLANE - STRIP :]
        z_down[:, :, lanes] = prim_z_ref[p, :, :, :STRIP]


def lane_at(value, k):
    width = value.shape[1]
    return pltpu.roll(value, (-k * EDGE) % width, 1)


def row_at(value, k):
    height = value.shape[0]
    return pltpu.roll(value, (-k) % height, 0)


def update_kernel(u_ref, prim_ref, prim_z_ref, x_low, x_high, y_low, y_high, z_low, z_high, out_ref, change_ref):
    slots = u_ref.shape[0]
    for p in range(slots):
        lanes = slice(p * STRIP, (p + 1) * STRIP)
        for half in range(2):
            rows = slice(half * 8, half * 8 + 8)
            lines = [
                jnp.concatenate([z_low[q, rows, lanes], prim_z_ref[p, q, rows, :], z_high[q, rows, lanes]], axis=1)
                for q in range(FIELDS)
            ]
            for q, value in enumerate(sweep(lines, 2, lane_at)):
                change_ref[p, q, rows, :] = value[:, STRIP : STRIP + PLANE]
    flat = change_ref[...].reshape(slots * FIELDS * EDGE, PLANE)
    change_ref[...] = exchange_lanes(flat).reshape(slots, FIELDS, EDGE, PLANE)
    for p in range(slots):
        lanes = slice(p * STRIP, (p + 1) * STRIP)
        for half in range(2):
            rows = slice(half * 8, half * 8 + 8)
            lines = [
                jnp.concatenate([y_low[q, rows, lanes], prim_ref[p, q, rows, :], y_high[q, rows, lanes]], axis=1)
                for q in range(FIELDS)
            ]
            for q, value in enumerate(sweep(lines, 1, lane_at)):
                change_ref[p, q, rows, :] += value[:, STRIP : STRIP + PLANE]
    for half in range(2):
        lanes = slice(half * 128, half * 128 + 128)
        lines = [
            jnp.concatenate(
                [x_low[q, :, lanes]] + [prim_ref[p, q, :, lanes] for p in range(slots)] + [x_high[q, :, lanes]], axis=0
            )
            for q in range(FIELDS)
        ]
        for q, value in enumerate(sweep(lines, 0, row_at)):
            for p in range(slots):
                first = GHOST + p * EDGE
                total = change_ref[p, q, :, lanes] + value[first : first + EDGE]
                out_ref[p, q, :, lanes] = u_ref[p, q, :, lanes] - STEP_RATIO * total


def place_kernel(index_ref, owner_ref, slot_ref, own_ref, partner_ref, out_ref):
    slots = own_ref.shape[0]
    me, group_place = index_ref[0], index_ref[1]
    first = (group_place // 2) * (2 * slots)
    low = group_place % 2 == 0
    out_ref[...] = jnp.zeros_like(out_ref)
    for member in range(2):
        for p in range(slots):
            k = first + member * slots + p
            owned = owner_ref[k] == me
            slot = jnp.where(owned, slot_ref[k], 0)
            mine = low if member == 0 else jnp.logical_not(low)

            @pl.when(jnp.logical_and(owned, mine))
            def _(slot=slot, p=p):
                out_ref[slot] = own_ref[p]

            @pl.when(jnp.logical_and(owned, jnp.logical_not(mine)))
            def _(slot=slot, p=p):
                out_ref[slot] = partner_ref[p]


def on_device(patches, new_owner, new_slot):
    slots = patches.shape[0]
    f32 = jnp.float32
    shape = jax.ShapeDtypeStruct
    block = shape((slots, FIELDS, EDGE, PLANE), f32)
    x_side = shape((FIELDS, GHOST, PLANE), f32)
    side = shape((FIELDS, EDGE, slots * STRIP), f32)
    prim, prim_z, x_up, x_down, y_up, y_down, z_up, z_down = pl.pallas_call(
        pack_kernel,
        out_shape=[block, block, x_side, x_side, side, side, side, side],
        in_specs=[VMEM],
        out_specs=[VMEM] * 8,
        name="pack",
    )(patches)

    def shift(value, axis, step):
        count = lax.axis_size(axis)
        return lax.ppermute(value, axis, [(i, (i + step) % count) for i in range(count)])

    z_low, z_high = shift(z_up, "gz", 1), shift(z_down, "gz", -1)
    y_low, y_high = shift(y_up, "gy", 1), shift(y_down, "gy", -1)
    x_low, x_high = shift(x_up, "gx", 1), shift(x_down, "gx", -1)
    advanced = pl.pallas_call(
        update_kernel,
        out_shape=block,
        in_specs=[VMEM] * 9,
        out_specs=VMEM,
        scratch_shapes=[pltpu.VMEM((slots, FIELDS, EDGE, PLANE), f32)],
        name="update",
    )(patches, prim, prim_z, x_low, x_high, y_low, y_high, z_low, z_high)
    members = lax.axis_size("gz")
    partner = lax.ppermute(advanced, "gz", [(i, i ^ 1) for i in range(members)])
    place = lax.axis_index("gz")
    me = (lax.axis_index("gx") * lax.axis_size("gy") + lax.axis_index("gy")) * members + place
    return pl.pallas_call(
        place_kernel,
        out_shape=shape((CAP, FIELDS, EDGE, PLANE), f32),
        in_specs=[SMEM, SMEM, SMEM, VMEM, VMEM],
        out_specs=VMEM,
        name="place",
    )(jnp.stack([me, place]).astype(jnp.int32), new_owner, new_slot, advanced, partner)


def solution(mesh):
    in_specs = (P(("gx", "gy", "gz"), None, None, None), P(("gx", "gy")), P(("gx", "gy")))
    out_specs = P(("gx", "gy", "gz"), None, None, None)
    return jax.shard_map(
        on_device, mesh=mesh, in_specs=in_specs, out_specs=out_specs, check_vma=False
    )
```

```python
import jax
import jax.numpy as jnp
from jax import lax
from jax.experimental import pallas as pl
from jax.experimental.pallas import tpu as pltpu
from jax.sharding import PartitionSpec as P

EDGE = 16
GHOST = 4
CAP = 4
FIELDS = 6
PLANE = EDGE * EDGE
STRIP = GHOST * EDGE
HALF = 128

STEP_RATIO = 0.08
VMEM = pl.BlockSpec(memory_space=pltpu.VMEM)
ANY = pl.BlockSpec(memory_space=pl.ANY)
SMEM = pl.BlockSpec(memory_space=pltpu.SMEM)


def to_primitive(u):
    density, mom_x, mom_y, mom_z, energy, species = u
    inverse = 1.0 / density
    vel_x, vel_y, vel_z = mom_x * inverse, mom_y * inverse, mom_z * inverse
    kinetic = 0.5 * (mom_x * vel_x + mom_y * vel_y + mom_z * vel_z)
    pressure = (2.0 / 3.0) * (energy - kinetic)
    return [density, vel_x, vel_y, vel_z, pressure, species * inverse]


def median_zero(second, third):
    return jnp.maximum(jnp.minimum(second, 0.0), jnp.minimum(jnp.maximum(second, 0.0), third))


def side_terms(state, normal):
    density, pressure = state[0], state[4]
    ratio = pressure / density
    speed = state[1 + normal]
    square = state[1] * state[1] + state[2] * state[2] + state[3] * state[3]
    specific = 1.5 * ratio + 0.5 * square
    signal = jnp.abs(speed) + jnp.sqrt((5.0 / 3.0) * ratio)
    return speed, specific, signal


def sweep(primitive, normal, at):
    plus, minus = [], []
    for value in primitive:
        after = at(value, 1)
        face = 37.0 * (value + after) - 8.0 * (at(value, -1) + at(value, 2)) + (at(value, -2) + at(value, 3))
        face = face * (1.0 / 60.0)
        face = jnp.minimum(jnp.maximum(face, jnp.minimum(value, after)), jnp.maximum(value, after))
        left_jump = value - at(face, -1)
        right_jump = face - value
        plus.append(value + median_zero(right_jump, 2.0 * left_jump))
        minus.append(at(value - median_zero(left_jump, 2.0 * right_jump), 1))
    left_speed, left_specific, left_signal = side_terms(plus, normal)
    right_speed, right_specific, right_signal = side_terms(minus, normal)
    signal = jnp.maximum(left_signal, right_signal)
    left_weight = 0.5 * plus[0] * (left_speed + signal)
    right_weight = 0.5 * minus[0] * (right_speed - signal)
    flux = [left_weight + right_weight]
    for k in (1, 2, 3):
        flux.append(left_weight * plus[k] + right_weight * minus[k])
    flux[1 + normal] = flux[1 + normal] + 0.5 * (plus[4] + minus[4])
    flux.append(
        left_weight * left_specific
        + right_weight * right_specific
        + 0.5 * (plus[4] * left_speed + minus[4] * right_speed)
    )
    flux.append(left_weight * plus[5] + right_weight * minus[5])
    return [f - at(f, -1) for f in flux]


def exchange_lanes(rows):
    source = lax.broadcasted_iota(jnp.int32, (PLANE, PLANE), 0)
    target = lax.broadcasted_iota(jnp.int32, (PLANE, PLANE), 1)
    wanted = (target % EDGE) * EDGE + target // EDGE
    swap = jnp.where(source == wanted, 1.0, 0.0).astype(jnp.bfloat16)
    total = None
    for _ in range(3):
        part = rows.astype(jnp.bfloat16)
        moved = jnp.dot(part, swap, preferred_element_type=jnp.float32)
        total = moved if total is None else total + moved
        rows = rows - part.astype(jnp.float32)
    return total


def to_lines(first, second):
    left = lax.broadcasted_iota(jnp.int32, (2 * EDGE, HALF), 1) < STRIP
    rows = []
    for part in range(2):
        one = first.reshape(2 * EDGE, PLANE)[:, part * HALF : (part + 1) * HALF]
        two = second.reshape(2 * EDGE, PLANE)[:, part * HALF : (part + 1) * HALF]
        rows.append(jnp.where(left, one, pltpu.roll(two, STRIP, 1)))
        rows.append(jnp.where(left, pltpu.roll(one, STRIP, 1), two))
    lines = jnp.concatenate(rows, axis=0).T
    return lines[:STRIP], lines[STRIP:]


def from_lines(first, second):
    left = lax.broadcasted_iota(jnp.int32, (2 * EDGE, HALF), 1) < STRIP
    rows = jnp.concatenate([first, second], axis=0).T
    rows = [rows[k * 2 * EDGE : (k + 1) * 2 * EDGE] for k in range(4)]
    one, two = [], []
    for part in range(2):
        low, high = rows[2 * part], rows[2 * part + 1]
        one.append(jnp.where(left, low, pltpu.roll(high, STRIP, 1)))
        two.append(jnp.where(left, pltpu.roll(low, STRIP, 1), high))
    return jnp.concatenate(one, axis=1), jnp.concatenate(two, axis=1)


def pack_kernel(u_ref, prim_ref, lines_z, lines_y, x_up, x_down, y_up, y_down, z_up, z_down):
    slots = u_ref.shape[0]
    for p in range(slots):
        for q, value in enumerate(to_primitive([u_ref[p, q] for q in range(FIELDS)])):
            prim_ref[p, q] = value
    x_up[...] = prim_ref[slots - 1, :, EDGE - GHOST :, :]
    x_down[...] = prim_ref[0, :, :GHOST, :]
    swapped = exchange_lanes(prim_ref[...].reshape(slots * FIELDS * EDGE, PLANE))
    swapped = swapped.reshape(slots, FIELDS, EDGE, PLANE)
    for pair in range(0, FIELDS, 2):
        for ref, pieces in (
            (lines_z, to_lines(prim_ref[:, pair], prim_ref[:, pair + 1])),
            (lines_y, to_lines(swapped[:, pair], swapped[:, pair + 1])),
        ):
            for k in range(2):
                ref[pair + k] = pieces[k].reshape(GHOST, EDGE, HALF)
    for ref, up, down in ((lines_z, z_up, z_down), (lines_y, y_up, y_down)):
        up[...] = ref[:, :, EDGE - GHOST :, :]
        down[...] = ref[:, :, :GHOST, :]


def row_at(value, k):
    height = value.shape[0]
    return pltpu.roll(value, (-k) % height, 0)


def sweep_lines(low, lines, high, normal, change):
    for group in range(GHOST):
        extended = [
            jnp.concatenate([low[q, group], lines[q, group], high[q, group]], axis=0) for q in range(FIELDS)
        ]
        for q, value in enumerate(sweep(extended, normal, row_at)):
            change[q, group] = value[GHOST : GHOST + EDGE]


def lines_kernel(lines_z, lines_y, z_low, z_high, y_low, y_high, out_ref, change_z, change_y):
    slots = out_ref.shape[0]
    sweep_lines(y_low, lines_y, y_high, 1, change_y)
    for pair in range(0, FIELDS, 2):
        parts = from_lines(change_y[pair].reshape(STRIP, HALF), change_y[pair + 1].reshape(STRIP, HALF))
        for k in range(2):
            out_ref[:, pair + k] = parts[k].reshape(slots, EDGE, PLANE)
    flat = out_ref[...].reshape(slots * FIELDS * EDGE, PLANE)
    out_ref[...] = exchange_lanes(flat).reshape(slots, FIELDS, EDGE, PLANE)
    sweep_lines(z_low, lines_z, z_high, 2, change_z)
    for pair in range(0, FIELDS, 2):
        parts = from_lines(change_z[pair].reshape(STRIP, HALF), change_z[pair + 1].reshape(STRIP, HALF))
        for k in range(2):
            out_ref[:, pair + k] += parts[k].reshape(slots, EDGE, PLANE)


def finish_kernel(u_ref, prim_ref, change_ref, x_low, x_high, out_ref):
    slots = u_ref.shape[0]
    for half in range(2):
        lanes = slice(half * HALF, half * HALF + HALF)
        lines = [
            jnp.concatenate(
                [x_low[q, :, lanes]] + [prim_ref[p, q, :, lanes] for p in range(slots)] + [x_high[q, :, lanes]], axis=0
            )
            for q in range(FIELDS)
        ]
        for q, value in enumerate(sweep(lines, 0, row_at)):
            for p in range(slots):
                first = GHOST + p * EDGE
                total = change_ref[p, q, :, lanes] + value[first : first + EDGE]
                out_ref[p, q, :, lanes] = u_ref[p, q, :, lanes] - STEP_RATIO * total


def place_kernel(index_ref, owner_ref, slot_ref, own_ref, partner_ref, out_ref, zeros, sems):
    slots = own_ref.shape[0]
    me, group_place = index_ref[0], index_ref[1]
    first = (group_place // 2) * (2 * slots)
    side = group_place % 2
    zeros[...] = jnp.zeros_like(zeros)
    for s in range(CAP):
        empty = True
        for member in range(2):
            for p in range(slots):
                k = first + member * slots + p
                here = jnp.logical_and(owner_ref[k] == me, slot_ref[k] == s)
                empty = jnp.logical_and(empty, jnp.logical_not(here))
                for ref, wanted in ((own_ref, side == member), (partner_ref, side != member)):

                    @pl.when(jnp.logical_and(here, wanted))
                    def _(ref=ref, p=p, s=s):
                        pltpu.make_async_copy(ref.at[p], out_ref.at[s], sems.at[s]).start()

        @pl.when(empty)
        def _(s=s):
            pltpu.make_async_copy(zeros, out_ref.at[s], sems.at[s]).start()

    for s in range(CAP):
        pltpu.make_async_copy(zeros, out_ref.at[s], sems.at[s]).wait()


def on_device(patches, new_owner, new_slot):
    slots = patches.shape[0]
    f32 = jnp.float32
    shape = jax.ShapeDtypeStruct
    block = shape((slots, FIELDS, EDGE, PLANE), f32)
    lines = shape((FIELDS, GHOST, EDGE, HALF), f32)
    x_side = shape((FIELDS, GHOST, PLANE), f32)
    side = shape((FIELDS, GHOST, GHOST, HALF), f32)
    prim, lines_z, lines_y, x_up, x_down, y_up, y_down, z_up, z_down = pl.pallas_call(
        pack_kernel,
        out_shape=[block, lines, lines, x_side, x_side, side, side, side, side],
        in_specs=[VMEM],
        out_specs=[VMEM] * 9,
        name="pack",
    )(patches)

    def shift(value, axis, step):
        count = lax.axis_size(axis)
        return lax.ppermute(value, axis, [(i, (i + step) % count) for i in range(count)])

    z_low, z_high = shift(z_up, "gz", 1), shift(z_down, "gz", -1)
    y_low, y_high = shift(y_up, "gy", 1), shift(y_down, "gy", -1)
    x_low, x_high = shift(x_up, "gx", 1), shift(x_down, "gx", -1)
    change = pl.pallas_call(
        lines_kernel,
        out_shape=block,
        in_specs=[VMEM] * 6,
        out_specs=VMEM,
        scratch_shapes=[pltpu.VMEM(lines.shape, f32)] * 2,
        name="lines",
    )(lines_z, lines_y, z_low, z_high, y_low, y_high)
    advanced = pl.pallas_call(
        finish_kernel, out_shape=block, in_specs=[VMEM] * 5, out_specs=VMEM, name="finish"
    )(patches, prim, change, x_low, x_high)
    members = lax.axis_size("gz")
    partner = lax.ppermute(advanced, "gz", [(i, i ^ 1) for i in range(members)])
    place = lax.axis_index("gz")
    me = (lax.axis_index("gx") * lax.axis_size("gy") + lax.axis_index("gy")) * members + place
    return pl.pallas_call(
        place_kernel,
        out_shape=shape((CAP, FIELDS, EDGE, PLANE), f32),
        in_specs=[SMEM, SMEM, SMEM, ANY, ANY],
        out_specs=ANY,
        scratch_shapes=[pltpu.VMEM((FIELDS, EDGE, PLANE), f32), pltpu.SemaphoreType.DMA((CAP,))],
        name="place",
    )(jnp.stack([me, place]).astype(jnp.int32), new_owner, new_slot, advanced, partner)


def solution(mesh):
    in_specs = (P(("gx", "gy", "gz"), None, None, None), P(("gx", "gy")), P(("gx", "gy")))
    out_specs = P(("gx", "gy", "gz"), None, None, None)
    return jax.shard_map(
        on_device, mesh=mesh, in_specs=in_specs, out_specs=out_specs, check_vma=False
    )
```

```python
import jax
import jax.numpy as jnp
from jax import lax
from jax.experimental import pallas as pl
from jax.experimental.pallas import tpu as pltpu
from jax.sharding import PartitionSpec as P

EDGE = 16
GHOST = 4
CAP = 4
FIELDS = 6
PLANE = EDGE * EDGE
STRIP = GHOST * EDGE
HALF = 128

STEP_RATIO = 0.08
VMEM = pl.BlockSpec(memory_space=pltpu.VMEM)
ANY = pl.BlockSpec(memory_space=pl.ANY)
PARAMS = pltpu.CompilerParams(vmem_limit_bytes=6 * 1024 * 1024)
SMEM = pl.BlockSpec(memory_space=pltpu.SMEM)


def to_primitive(u):
    density, mom_x, mom_y, mom_z, energy, species = u
    inverse = 1.0 / density
    vel_x, vel_y, vel_z = mom_x * inverse, mom_y * inverse, mom_z * inverse
    kinetic = 0.5 * (mom_x * vel_x + mom_y * vel_y + mom_z * vel_z)
    pressure = (2.0 / 3.0) * (energy - kinetic)
    return [density, vel_x, vel_y, vel_z, pressure, species * inverse]


def median_zero(second, third):
    return jnp.maximum(jnp.minimum(second, 0.0), jnp.minimum(jnp.maximum(second, 0.0), third))


def side_terms(state, normal):
    density, pressure = state[0], state[4]
    ratio = pressure / density
    speed = state[1 + normal]
    square = state[1] * state[1] + state[2] * state[2] + state[3] * state[3]
    specific = 1.5 * ratio + 0.5 * square
    signal = jnp.abs(speed) + jnp.sqrt((5.0 / 3.0) * ratio)
    return speed, specific, signal


def sweep(primitive, normal, at):
    plus, minus = [], []
    for value in primitive:
        after = at(value, 1)
        face = 37.0 * (value + after) - 8.0 * (at(value, -1) + at(value, 2)) + (at(value, -2) + at(value, 3))
        face = face * (1.0 / 60.0)
        face = jnp.minimum(jnp.maximum(face, jnp.minimum(value, after)), jnp.maximum(value, after))
        left_jump = value - at(face, -1)
        right_jump = face - value
        plus.append(value + median_zero(right_jump, 2.0 * left_jump))
        minus.append(at(value - median_zero(left_jump, 2.0 * right_jump), 1))
    left_speed, left_specific, left_signal = side_terms(plus, normal)
    right_speed, right_specific, right_signal = side_terms(minus, normal)
    signal = jnp.maximum(left_signal, right_signal)
    left_weight = 0.5 * plus[0] * (left_speed + signal)
    right_weight = 0.5 * minus[0] * (right_speed - signal)
    flux = [left_weight + right_weight]
    for k in (1, 2, 3):
        flux.append(left_weight * plus[k] + right_weight * minus[k])
    flux[1 + normal] = flux[1 + normal] + 0.5 * (plus[4] + minus[4])
    flux.append(
        left_weight * left_specific
        + right_weight * right_specific
        + 0.5 * (plus[4] * left_speed + minus[4] * right_speed)
    )
    flux.append(left_weight * plus[5] + right_weight * minus[5])
    return [f - at(f, -1) for f in flux]


def exchange_lanes(rows):
    source = lax.broadcasted_iota(jnp.int32, (PLANE, PLANE), 0)
    target = lax.broadcasted_iota(jnp.int32, (PLANE, PLANE), 1)
    wanted = (target % EDGE) * EDGE + target // EDGE
    swap = jnp.where(source == wanted, 1.0, 0.0).astype(jnp.bfloat16)
    total = None
    for _ in range(3):
        part = rows.astype(jnp.bfloat16)
        moved = jnp.dot(part, swap, preferred_element_type=jnp.float32)
        total = moved if total is None else total + moved
        rows = rows - part.astype(jnp.float32)
    return total


def to_lines(first, second):
    left = lax.broadcasted_iota(jnp.int32, (2 * EDGE, HALF), 1) < STRIP
    rows = []
    for part in range(2):
        one = first.reshape(2 * EDGE, PLANE)[:, part * HALF : (part + 1) * HALF]
        two = second.reshape(2 * EDGE, PLANE)[:, part * HALF : (part + 1) * HALF]
        rows.append(jnp.where(left, one, pltpu.roll(two, STRIP, 1)))
        rows.append(jnp.where(left, pltpu.roll(one, STRIP, 1), two))
    lines = jnp.concatenate(rows, axis=0).T
    return lines[:STRIP], lines[STRIP:]


def from_lines(first, second):
    left = lax.broadcasted_iota(jnp.int32, (2 * EDGE, HALF), 1) < STRIP
    rows = jnp.concatenate([first, second], axis=0).T
    rows = [rows[k * 2 * EDGE : (k + 1) * 2 * EDGE] for k in range(4)]
    one, two = [], []
    for part in range(2):
        low, high = rows[2 * part], rows[2 * part + 1]
        one.append(jnp.where(left, low, pltpu.roll(high, STRIP, 1)))
        two.append(jnp.where(left, pltpu.roll(low, STRIP, 1), high))
    return jnp.concatenate(one, axis=1), jnp.concatenate(two, axis=1)


def pack_kernel(u_ref, prim_ref, lines_z, lines_y, x_up, x_down, y_up, y_down, z_up, z_down):
    slots = u_ref.shape[0]
    for p in range(slots):
        for q, value in enumerate(to_primitive([u_ref[p, q] for q in range(FIELDS)])):
            prim_ref[p, q] = value
    x_up[...] = prim_ref[slots - 1, :, EDGE - GHOST :, :]
    x_down[...] = prim_ref[0, :, :GHOST, :]
    swapped = exchange_lanes(prim_ref[...].reshape(slots * FIELDS * EDGE, PLANE))
    swapped = swapped.reshape(slots, FIELDS, EDGE, PLANE)
    for pair in range(0, FIELDS, 2):
        for ref, pieces in (
            (lines_z, to_lines(prim_ref[:, pair], prim_ref[:, pair + 1])),
            (lines_y, to_lines(swapped[:, pair], swapped[:, pair + 1])),
        ):
            for k in range(2):
                ref[pair + k] = pieces[k].reshape(GHOST, EDGE, HALF)
    for ref, up, down in ((lines_z, z_up, z_down), (lines_y, y_up, y_down)):
        up[...] = ref[:, :, EDGE - GHOST :, :]
        down[...] = ref[:, :, :GHOST, :]


def row_at(value, k):
    height = value.shape[0]
    return pltpu.roll(value, (-k) % height, 0)


def sweep_lines(low, lines, high, normal, change):
    for group in range(GHOST):
        extended = [
            jnp.concatenate([low[q, group], lines[q, group], high[q, group]], axis=0) for q in range(FIELDS)
        ]
        for q, value in enumerate(sweep(extended, normal, row_at)):
            change[q, group] = value[GHOST : GHOST + EDGE]


def sides_kernel(prim_ref, lines_y, x_low, x_high, y_low, y_high, out_ref, change_y):
    slots = out_ref.shape[0]
    sweep_lines(y_low, lines_y, y_high, 1, change_y)
    for pair in range(0, FIELDS, 2):
        parts = from_lines(change_y[pair].reshape(STRIP, HALF), change_y[pair + 1].reshape(STRIP, HALF))
        for k in range(2):
            out_ref[:, pair + k] = parts[k].reshape(slots, EDGE, PLANE)
    flat = out_ref[...].reshape(slots * FIELDS * EDGE, PLANE)
    out_ref[...] = exchange_lanes(flat).reshape(slots, FIELDS, EDGE, PLANE)
    for half in range(2):
        lanes = slice(half * HALF, half * HALF + HALF)
        lines = [
            jnp.concatenate(
                [x_low[q, :, lanes]] + [prim_ref[p, q, :, lanes] for p in range(slots)] + [x_high[q, :, lanes]], axis=0
            )
            for q in range(FIELDS)
        ]
        for q, value in enumerate(sweep(lines, 0, row_at)):
            for p in range(slots):
                first = GHOST + p * EDGE
                out_ref[p, q, :, lanes] += value[first : first + EDGE]


def finish_kernel(u_ref, change_ref, lines_z, z_low, z_high, out_ref, change_z):
    slots = u_ref.shape[0]
    sweep_lines(z_low, lines_z, z_high, 2, change_z)
    for pair in range(0, FIELDS, 2):
        parts = from_lines(change_z[pair].reshape(STRIP, HALF), change_z[pair + 1].reshape(STRIP, HALF))
        for k in range(2):
            total = change_ref[:, pair + k] + parts[k].reshape(slots, EDGE, PLANE)
            out_ref[:, pair + k] = u_ref[:, pair + k] - STEP_RATIO * total


def place_kernel(index_ref, owner_ref, slot_ref, own_ref, partner_ref, out_ref, zeros, sems):
    slots = own_ref.shape[0]
    me, group_place = index_ref[0], index_ref[1]
    first = (group_place // 2) * (2 * slots)
    side = group_place % 2
    zeros[...] = jnp.zeros_like(zeros)
    for s in range(CAP):
        empty = True
        for member in range(2):
            for p in range(slots):
                k = first + member * slots + p
                here = jnp.logical_and(owner_ref[k] == me, slot_ref[k] == s)
                empty = jnp.logical_and(empty, jnp.logical_not(here))
                for ref, wanted in ((own_ref, side == member), (partner_ref, side != member)):

                    @pl.when(jnp.logical_and(here, wanted))
                    def _(ref=ref, p=p, s=s):
                        pltpu.make_async_copy(ref.at[p], out_ref.at[s], sems.at[s]).start()

        @pl.when(empty)
        def _(s=s):
            pltpu.make_async_copy(zeros, out_ref.at[s], sems.at[s]).start()

    for s in range(CAP):
        pltpu.make_async_copy(zeros, out_ref.at[s], sems.at[s]).wait()


def on_device(patches, new_owner, new_slot):
    slots = patches.shape[0]
    f32 = jnp.float32
    shape = jax.ShapeDtypeStruct
    block = shape((slots, FIELDS, EDGE, PLANE), f32)
    lines = shape((FIELDS, GHOST, EDGE, HALF), f32)
    x_side = shape((FIELDS, GHOST, PLANE), f32)
    side = shape((FIELDS, GHOST, GHOST, HALF), f32)
    prim, lines_z, lines_y, x_up, x_down, y_up, y_down, z_up, z_down = pl.pallas_call(
        pack_kernel,
        out_shape=[block, lines, lines, x_side, x_side, side, side, side, side],
        in_specs=[VMEM],
        out_specs=[VMEM] * 9,
        compiler_params=PARAMS,
        name="pack",
    )(patches)

    def shift(value, axis, step):
        count = lax.axis_size(axis)
        return lax.ppermute(value, axis, [(i, (i + step) % count) for i in range(count)])

    x_low, x_high = shift(x_up, "gx", 1), shift(x_down, "gx", -1)
    y_low, y_high = shift(y_up, "gy", 1), shift(y_down, "gy", -1)
    z_low, z_high = shift(z_up, "gz", 1), shift(z_down, "gz", -1)
    change = pl.pallas_call(
        sides_kernel,
        out_shape=block,
        in_specs=[VMEM] * 6,
        out_specs=VMEM,
        scratch_shapes=[pltpu.VMEM(lines.shape, f32)],
        compiler_params=PARAMS,
        name="sides",
    )(prim, lines_y, x_low, x_high, y_low, y_high)
    advanced = pl.pallas_call(
        finish_kernel,
        out_shape=block,
        in_specs=[VMEM] * 5,
        out_specs=VMEM,
        scratch_shapes=[pltpu.VMEM(lines.shape, f32)],
        compiler_params=PARAMS,
        name="finish",
    )(patches, change, lines_z, z_low, z_high)
    members = lax.axis_size("gz")
    partner = lax.ppermute(advanced, "gz", [(i, i ^ 1) for i in range(members)])
    place = lax.axis_index("gz")
    me = (lax.axis_index("gx") * lax.axis_size("gy") + lax.axis_index("gy")) * members + place
    return pl.pallas_call(
        place_kernel,
        out_shape=shape((CAP, FIELDS, EDGE, PLANE), f32),
        in_specs=[SMEM, SMEM, SMEM, VMEM, VMEM],
        out_specs=ANY,
        scratch_shapes=[pltpu.VMEM((FIELDS, EDGE, PLANE), f32), pltpu.SemaphoreType.DMA((CAP,))],
        compiler_params=PARAMS,
        name="place",
    )(jnp.stack([me, place]).astype(jnp.int32), new_owner, new_slot, advanced, partner)


def solution(mesh):
    in_specs = (P(("gx", "gy", "gz"), None, None, None), P(("gx", "gy")), P(("gx", "gy")))
    out_specs = P(("gx", "gy", "gz"), None, None, None)
    return jax.shard_map(
        on_device, mesh=mesh, in_specs=in_specs, out_specs=out_specs, check_vma=False
    )
```

```python
import jax
import jax.numpy as jnp
from jax import lax
from jax.experimental import pallas as pl
from jax.experimental.pallas import tpu as pltpu
from jax.sharding import PartitionSpec as P

EDGE = 16
GHOST = 4
CAP = 4
FIELDS = 6
PLANE = EDGE * EDGE
STRIP = GHOST * EDGE
HALF = 128

STEP_RATIO = 0.08
VMEM = pl.BlockSpec(memory_space=pltpu.VMEM)
ANY = pl.BlockSpec(memory_space=pl.ANY)
PARAMS = pltpu.CompilerParams(vmem_limit_bytes=6 * 1024 * 1024)
SMEM = pl.BlockSpec(memory_space=pltpu.SMEM)


def to_primitive(u):
    density, mom_x, mom_y, mom_z, energy, species = u
    inverse = 1.0 / density
    vel_x, vel_y, vel_z = mom_x * inverse, mom_y * inverse, mom_z * inverse
    kinetic = 0.5 * (mom_x * vel_x + mom_y * vel_y + mom_z * vel_z)
    pressure = (2.0 / 3.0) * (energy - kinetic)
    return [density, vel_x, vel_y, vel_z, pressure, species * inverse]


def median_zero(second, third):
    return jnp.maximum(jnp.minimum(second, 0.0), jnp.minimum(jnp.maximum(second, 0.0), third))


def side_terms(state, normal):
    density, pressure = state[0], state[4]
    ratio = pressure / density
    speed = state[1 + normal]
    square = state[1] * state[1] + state[2] * state[2] + state[3] * state[3]
    specific = 1.5 * ratio + 0.5 * square
    signal = jnp.abs(speed) + jnp.sqrt((5.0 / 3.0) * ratio)
    return speed, specific, signal


def sweep(primitive, normal, at):
    plus, minus = [], []
    for value in primitive:
        after = at(value, 1)
        face = 37.0 * (value + after) - 8.0 * (at(value, -1) + at(value, 2)) + (at(value, -2) + at(value, 3))
        face = face * (1.0 / 60.0)
        face = jnp.minimum(jnp.maximum(face, jnp.minimum(value, after)), jnp.maximum(value, after))
        left_jump = value - at(face, -1)
        right_jump = face - value
        plus.append(value + median_zero(right_jump, 2.0 * left_jump))
        minus.append(at(value - median_zero(left_jump, 2.0 * right_jump), 1))
    left_speed, left_specific, left_signal = side_terms(plus, normal)
    right_speed, right_specific, right_signal = side_terms(minus, normal)
    signal = jnp.maximum(left_signal, right_signal)
    left_weight = 0.5 * plus[0] * (left_speed + signal)
    right_weight = 0.5 * minus[0] * (right_speed - signal)
    flux = [left_weight + right_weight]
    for k in (1, 2, 3):
        flux.append(left_weight * plus[k] + right_weight * minus[k])
    flux[1 + normal] = flux[1 + normal] + 0.5 * (plus[4] + minus[4])
    flux.append(
        left_weight * left_specific
        + right_weight * right_specific
        + 0.5 * (plus[4] * left_speed + minus[4] * right_speed)
    )
    flux.append(left_weight * plus[5] + right_weight * minus[5])
    return [f - at(f, -1) for f in flux]


def exchange_lanes(rows):
    source = lax.broadcasted_iota(jnp.int32, (PLANE, PLANE), 0)
    target = lax.broadcasted_iota(jnp.int32, (PLANE, PLANE), 1)
    wanted = (target % EDGE) * EDGE + target // EDGE
    swap = jnp.where(source == wanted, 1.0, 0.0).astype(jnp.bfloat16)
    total = None
    for _ in range(3):
        part = rows.astype(jnp.bfloat16)
        moved = jnp.dot(part, swap, preferred_element_type=jnp.float32)
        total = moved if total is None else total + moved
        rows = rows - part.astype(jnp.float32)
    return total


def to_lines(first, second):
    left = lax.broadcasted_iota(jnp.int32, (2 * EDGE, HALF), 1) < STRIP
    rows = []
    for part in range(2):
        one = first.reshape(2 * EDGE, PLANE)[:, part * HALF : (part + 1) * HALF]
        two = second.reshape(2 * EDGE, PLANE)[:, part * HALF : (part + 1) * HALF]
        rows.append(jnp.where(left, one, pltpu.roll(two, STRIP, 1)))
        rows.append(jnp.where(left, pltpu.roll(one, STRIP, 1), two))
    lines = jnp.concatenate(rows, axis=0).T
    return lines[:STRIP], lines[STRIP:]


def from_lines(first, second):
    left = lax.broadcasted_iota(jnp.int32, (2 * EDGE, HALF), 1) < STRIP
    rows = jnp.concatenate([first, second], axis=0).T
    rows = [rows[k * 2 * EDGE : (k + 1) * 2 * EDGE] for k in range(4)]
    one, two = [], []
    for part in range(2):
        low, high = rows[2 * part], rows[2 * part + 1]
        one.append(jnp.where(left, low, pltpu.roll(high, STRIP, 1)))
        two.append(jnp.where(left, pltpu.roll(low, STRIP, 1), high))
    return jnp.concatenate(one, axis=1), jnp.concatenate(two, axis=1)


def pack_kernel(u_ref, prim_ref, lines_z, lines_y, x_up, x_down, y_up, y_down, z_up, z_down):
    slots = u_ref.shape[0]
    for p in range(slots):
        for q, value in enumerate(to_primitive([u_ref[p, q] for q in range(FIELDS)])):
            prim_ref[p, q] = value
    x_up[...] = prim_ref[slots - 1, :, EDGE - GHOST :, :]
    x_down[...] = prim_ref[0, :, :GHOST, :]
    swapped = exchange_lanes(prim_ref[...].reshape(slots * FIELDS * EDGE, PLANE))
    swapped = swapped.reshape(slots, FIELDS, EDGE, PLANE)
    for pair in range(0, FIELDS, 2):
        for ref, pieces in (
            (lines_z, to_lines(prim_ref[:, pair], prim_ref[:, pair + 1])),
            (lines_y, to_lines(swapped[:, pair], swapped[:, pair + 1])),
        ):
            for k in range(2):
                ref[pair + k] = pieces[k].reshape(GHOST, EDGE, HALF)
    for ref, up, down in ((lines_z, z_up, z_down), (lines_y, y_up, y_down)):
        up[...] = ref[:, :, EDGE - GHOST :, :]
        down[...] = ref[:, :, :GHOST, :]


def row_at(value, k):
    height = value.shape[0]
    return pltpu.roll(value, (-k) % height, 0)


def sweep_lines(low, lines, high, normal, change):
    for group in range(GHOST):
        extended = [
            jnp.concatenate([low[q, group], lines[q, group], high[q, group]], axis=0) for q in range(FIELDS)
        ]
        for q, value in enumerate(sweep(extended, normal, row_at)):
            change[q, group] = value[GHOST : GHOST + EDGE]


def sides_kernel(prim_ref, lines_y, x_low, x_high, y_low, y_high, out_ref, change_y):
    slots = out_ref.shape[0]
    sweep_lines(y_low, lines_y, y_high, 1, change_y)
    for pair in range(0, FIELDS, 2):
        parts = from_lines(change_y[pair].reshape(STRIP, HALF), change_y[pair + 1].reshape(STRIP, HALF))
        for k in range(2):
            out_ref[:, pair + k] = parts[k].reshape(slots, EDGE, PLANE)
    flat = out_ref[...].reshape(slots * FIELDS * EDGE, PLANE)
    out_ref[...] = exchange_lanes(flat).reshape(slots, FIELDS, EDGE, PLANE)
    for half in range(2):
        lanes = slice(half * HALF, half * HALF + HALF)
        lines = [
            jnp.concatenate(
                [x_low[q, :, lanes]] + [prim_ref[p, q, :, lanes] for p in range(slots)] + [x_high[q, :, lanes]], axis=0
            )
            for q in range(FIELDS)
        ]
        for q, value in enumerate(sweep(lines, 0, row_at)):
            for p in range(slots):
                first = GHOST + p * EDGE
                out_ref[p, q, :, lanes] += value[first : first + EDGE]


def finish_kernel(u_ref, change_ref, lines_z, z_low, z_high, out_ref, change_z):
    slots = u_ref.shape[0]
    sweep_lines(z_low, lines_z, z_high, 2, change_z)
    for pair in range(0, FIELDS, 2):
        parts = from_lines(change_z[pair].reshape(STRIP, HALF), change_z[pair + 1].reshape(STRIP, HALF))
        for k in range(2):
            total = change_ref[:, pair + k] + parts[k].reshape(slots, EDGE, PLANE)
            out_ref[:, pair + k] = u_ref[:, pair + k] - STEP_RATIO * total


def place_kernel(code_ref, own_ref, partner_ref, out_ref, zeros, sems):
    slots = own_ref.shape[0]
    zeros[...] = jnp.zeros_like(zeros)
    sources = [zeros] + [own_ref.at[p] for p in range(slots)] + [partner_ref.at[p] for p in range(slots)]
    for s in range(CAP):
        for c, source in enumerate(sources):

            @pl.when(code_ref[s] == c)
            def _(source=source, s=s):
                pltpu.make_async_copy(source, out_ref.at[s], sems.at[s]).start()

    for s in range(CAP):
        pltpu.make_async_copy(zeros, out_ref.at[s], sems.at[s]).wait()


def slot_codes(new_owner, new_slot, slots):
    members = lax.axis_size("gz")
    place = lax.axis_index("gz")
    me = (lax.axis_index("gx") * lax.axis_size("gy") + lax.axis_index("gy")) * members + place
    patch = lax.broadcasted_iota(jnp.int32, (CAP, members * slots), 1)
    slot = lax.broadcasted_iota(jnp.int32, (CAP, members * slots), 0)
    code = patch % slots + 1 + jnp.where(patch // slots == place, 0, slots)
    here = jnp.logical_and(new_owner[None, :] == me, new_slot[None, :] == slot)
    return jnp.sum(jnp.where(here, code, 0), axis=1)


def on_device(patches, new_owner, new_slot):
    slots = patches.shape[0]
    f32 = jnp.float32
    shape = jax.ShapeDtypeStruct
    block = shape((slots, FIELDS, EDGE, PLANE), f32)
    lines = shape((FIELDS, GHOST, EDGE, HALF), f32)
    x_side = shape((FIELDS, GHOST, PLANE), f32)
    side = shape((FIELDS, GHOST, GHOST, HALF), f32)
    prim, lines_z, lines_y, x_up, x_down, y_up, y_down, z_up, z_down = pl.pallas_call(
        pack_kernel,
        out_shape=[block, lines, lines, x_side, x_side, side, side, side, side],
        in_specs=[VMEM],
        out_specs=[VMEM] * 9,
        compiler_params=PARAMS,
        name="pack",
    )(patches)

    def shift(value, axis, step):
        count = lax.axis_size(axis)
        return lax.ppermute(value, axis, [(i, (i + step) % count) for i in range(count)])

    y_low = shift(y_up, "gy", 1)
    y_high = shift(y_down, "gy", -1)
    x_low = shift(x_up, "gx", 1)
    x_high = shift(x_down, "gx", -1)
    z_up, z_down, y_high = lax.optimization_barrier((z_up, z_down, y_high))
    z_low = shift(z_up, "gz", 1)
    z_high = shift(z_down, "gz", -1)
    change = pl.pallas_call(
        sides_kernel,
        out_shape=block,
        in_specs=[VMEM] * 6,
        out_specs=VMEM,
        scratch_shapes=[pltpu.VMEM(lines.shape, f32)],
        compiler_params=PARAMS,
        name="sides",
    )(prim, lines_y, x_low, x_high, y_low, y_high)
    advanced = pl.pallas_call(
        finish_kernel,
        out_shape=block,
        in_specs=[VMEM] * 5,
        out_specs=VMEM,
        scratch_shapes=[pltpu.VMEM(lines.shape, f32)],
        compiler_params=PARAMS,
        name="finish",
    )(patches, change, lines_z, z_low, z_high)
    advanced, new_owner, new_slot = lax.optimization_barrier((advanced, new_owner, new_slot))
    members = lax.axis_size("gz")
    partner = lax.ppermute(advanced, "gz", [(i, i ^ 1) for i in range(members)])
    return pl.pallas_call(
        place_kernel,
        out_shape=shape((CAP, FIELDS, EDGE, PLANE), f32),
        in_specs=[SMEM, VMEM, VMEM],
        out_specs=ANY,
        scratch_shapes=[pltpu.VMEM((FIELDS, EDGE, PLANE), f32), pltpu.SemaphoreType.DMA((CAP,))],
        compiler_params=PARAMS,
        name="place",
    )(slot_codes(new_owner, new_slot, slots), advanced, partner)


def solution(mesh):
    in_specs = (P(("gx", "gy", "gz"), None, None, None), P(("gx", "gy")), P(("gx", "gy")))
    out_specs = P(("gx", "gy", "gz"), None, None, None)
    return jax.shard_map(
        on_device, mesh=mesh, in_specs=in_specs, out_specs=out_specs, check_vma=False
    )
```

```python
import jax
import jax.numpy as jnp
from jax import lax
from jax.experimental import pallas as pl
from jax.experimental.pallas import tpu as pltpu
from jax.sharding import PartitionSpec as P

EDGE = 16
GHOST = 4
CAP = 4
FIELDS = 6
PLANE = EDGE * EDGE
STRIP = GHOST * EDGE
HALF = 128

STEP_RATIO = 0.08
VMEM = pl.BlockSpec(memory_space=pltpu.VMEM)
ANY = pl.BlockSpec(memory_space=pl.ANY)
PARAMS = pltpu.CompilerParams(vmem_limit_bytes=6 * 1024 * 1024)


def to_primitive(u):
    density, mom_x, mom_y, mom_z, energy, species = u
    inverse = 1.0 / density
    vel_x, vel_y, vel_z = mom_x * inverse, mom_y * inverse, mom_z * inverse
    kinetic = 0.5 * (mom_x * vel_x + mom_y * vel_y + mom_z * vel_z)
    pressure = (2.0 / 3.0) * (energy - kinetic)
    return [density, vel_x, vel_y, vel_z, pressure, species * inverse]


def median_zero(second, third):
    return jnp.maximum(jnp.minimum(second, 0.0), jnp.minimum(jnp.maximum(second, 0.0), third))


def side_terms(state, normal):
    density, pressure = state[0], state[4]
    ratio = pressure / density
    speed = state[1 + normal]
    square = state[1] * state[1] + state[2] * state[2] + state[3] * state[3]
    specific = 1.5 * ratio + 0.5 * square
    signal = jnp.abs(speed) + jnp.sqrt((5.0 / 3.0) * ratio)
    return speed, specific, signal


def sweep(primitive, normal, at):
    plus, minus = [], []
    for value in primitive:
        after = at(value, 1)
        face = 37.0 * (value + after) - 8.0 * (at(value, -1) + at(value, 2)) + (at(value, -2) + at(value, 3))
        face = face * (1.0 / 60.0)
        face = jnp.minimum(jnp.maximum(face, jnp.minimum(value, after)), jnp.maximum(value, after))
        left_jump = value - at(face, -1)
        right_jump = face - value
        plus.append(value + median_zero(right_jump, 2.0 * left_jump))
        minus.append(at(value - median_zero(left_jump, 2.0 * right_jump), 1))
    left_speed, left_specific, left_signal = side_terms(plus, normal)
    right_speed, right_specific, right_signal = side_terms(minus, normal)
    signal = jnp.maximum(left_signal, right_signal)
    left_weight = 0.5 * plus[0] * (left_speed + signal)
    right_weight = 0.5 * minus[0] * (right_speed - signal)
    flux = [left_weight + right_weight]
    for k in (1, 2, 3):
        flux.append(left_weight * plus[k] + right_weight * minus[k])
    flux[1 + normal] = flux[1 + normal] + 0.5 * (plus[4] + minus[4])
    flux.append(
        left_weight * left_specific
        + right_weight * right_specific
        + 0.5 * (plus[4] * left_speed + minus[4] * right_speed)
    )
    flux.append(left_weight * plus[5] + right_weight * minus[5])
    return [f - at(f, -1) for f in flux]


def exchange_lanes(rows):
    source = lax.broadcasted_iota(jnp.int32, (PLANE, PLANE), 0)
    target = lax.broadcasted_iota(jnp.int32, (PLANE, PLANE), 1)
    wanted = (target % EDGE) * EDGE + target // EDGE
    swap = jnp.where(source == wanted, 1.0, 0.0).astype(jnp.bfloat16)
    total = None
    for _ in range(3):
        part = rows.astype(jnp.bfloat16)
        moved = jnp.dot(part, swap, preferred_element_type=jnp.float32)
        total = moved if total is None else total + moved
        rows = rows - part.astype(jnp.float32)
    return total


def to_lines(first, second):
    left = lax.broadcasted_iota(jnp.int32, (2 * EDGE, HALF), 1) < STRIP
    rows = []
    for part in range(2):
        one = first.reshape(2 * EDGE, PLANE)[:, part * HALF : (part + 1) * HALF]
        two = second.reshape(2 * EDGE, PLANE)[:, part * HALF : (part + 1) * HALF]
        rows.append(jnp.where(left, one, pltpu.roll(two, STRIP, 1)))
        rows.append(jnp.where(left, pltpu.roll(one, STRIP, 1), two))
    lines = jnp.concatenate(rows, axis=0).T
    return lines[:STRIP], lines[STRIP:]


def from_lines(first, second):
    left = lax.broadcasted_iota(jnp.int32, (2 * EDGE, HALF), 1) < STRIP
    rows = jnp.concatenate([first, second], axis=0).T
    rows = [rows[k * 2 * EDGE : (k + 1) * 2 * EDGE] for k in range(4)]
    one, two = [], []
    for part in range(2):
        low, high = rows[2 * part], rows[2 * part + 1]
        one.append(jnp.where(left, low, pltpu.roll(high, STRIP, 1)))
        two.append(jnp.where(left, pltpu.roll(low, STRIP, 1), high))
    return jnp.concatenate(one, axis=1), jnp.concatenate(two, axis=1)


def pack_kernel(u_ref, prim_ref, lines_z, lines_y, y_up, y_down, z_up, z_down):
    slots = u_ref.shape[0]
    for p in range(slots):
        for q, value in enumerate(to_primitive([u_ref[p, q] for q in range(FIELDS)])):
            prim_ref[p, q] = value
    swapped = exchange_lanes(prim_ref[...].reshape(slots * FIELDS * EDGE, PLANE))
    swapped = swapped.reshape(slots, FIELDS, EDGE, PLANE)
    for pair in range(0, FIELDS, 2):
        for ref, pieces in (
            (lines_z, to_lines(prim_ref[:, pair], prim_ref[:, pair + 1])),
            (lines_y, to_lines(swapped[:, pair], swapped[:, pair + 1])),
        ):
            for k in range(2):
                ref[pair + k] = pieces[k].reshape(GHOST, EDGE, HALF)
    for ref, up, down in ((lines_z, z_up, z_down), (lines_y, y_up, y_down)):
        up[...] = ref[:, :, EDGE - GHOST :, :]
        down[...] = ref[:, :, :GHOST, :]


def row_at(value, k):
    height = value.shape[0]
    return pltpu.roll(value, (-k) % height, 0)


def sweep_lines(low, lines, high, normal, change):
    for group in range(GHOST):
        extended = [
            jnp.concatenate([low[q, group], lines[q, group], high[q, group]], axis=0) for q in range(FIELDS)
        ]
        for q, value in enumerate(sweep(extended, normal, row_at)):
            change[q, group] = value[GHOST : GHOST + EDGE]


def rows_kernel(prim_ref, low_ref, high_ref, out_ref):
    slots = out_ref.shape[0]
    for half in range(2):
        lanes = slice(half * HALF, half * HALF + HALF)
        low = to_primitive([low_ref[slots - 1, q, EDGE - GHOST :, lanes] for q in range(FIELDS)])
        high = to_primitive([high_ref[0, q, :GHOST, lanes] for q in range(FIELDS)])
        lines = [
            jnp.concatenate([low[q]] + [prim_ref[p, q, :, lanes] for p in range(slots)] + [high[q]], axis=0)
            for q in range(FIELDS)
        ]
        for q, value in enumerate(sweep(lines, 0, row_at)):
            for p in range(slots):
                first = GHOST + p * EDGE
                out_ref[p, q, :, lanes] = value[first : first + EDGE]


def columns_kernel(before_ref, lines_y, y_low, y_high, out_ref, change_y):
    slots = out_ref.shape[0]
    sweep_lines(y_low, lines_y, y_high, 1, change_y)
    for pair in range(0, FIELDS, 2):
        parts = from_lines(change_y[pair].reshape(STRIP, HALF), change_y[pair + 1].reshape(STRIP, HALF))
        for k in range(2):
            out_ref[:, pair + k] = parts[k].reshape(slots, EDGE, PLANE)
    flat = exchange_lanes(out_ref[...].reshape(slots * FIELDS * EDGE, PLANE))
    out_ref[...] = flat.reshape(slots, FIELDS, EDGE, PLANE) + before_ref[...]


def finish_kernel(u_ref, change_ref, lines_z, z_low, z_high, out_ref, change_z):
    slots = u_ref.shape[0]
    sweep_lines(z_low, lines_z, z_high, 2, change_z)
    for pair in range(0, FIELDS, 2):
        parts = from_lines(change_z[pair].reshape(STRIP, HALF), change_z[pair + 1].reshape(STRIP, HALF))
        for k in range(2):
            total = change_ref[:, pair + k] + parts[k].reshape(slots, EDGE, PLANE)
            out_ref[:, pair + k] = u_ref[:, pair + k] - STEP_RATIO * total


def place_kernel(code_ref, own_ref, partner_ref, out_ref, held, sems):
    slots = own_ref.shape[0]
    copies = []
    for s in range(CAP):
        code = jnp.concatenate([code_ref[s]] * 2, axis=1)
        for q in range(FIELDS):
            for half in range(2):
                rows = slice(half * 8, half * 8 + 8)
                value = jnp.zeros((8, PLANE), jnp.float32)
                for p in range(slots):
                    value = jnp.where(code == 1 + p, own_ref[p, q, rows, :], value)
                    value = jnp.where(code == 1 + slots + p, partner_ref[p, q, rows, :], value)
                held[s, q, rows, :] = value
        copies.append(pltpu.make_async_copy(held.at[s], out_ref.at[s], sems.at[s]))
        copies[s].start()
    for copy in copies:
        copy.wait()


def slot_codes(new_owner, new_slot, slots):
    members = lax.axis_size("gz")
    place = lax.axis_index("gz")
    me = (lax.axis_index("gx") * lax.axis_size("gy") + lax.axis_index("gy")) * members + place
    patch = lax.broadcasted_iota(jnp.int32, (CAP, members * slots), 1)
    slot = lax.broadcasted_iota(jnp.int32, (CAP, members * slots), 0)
    code = patch % slots + 1 + jnp.where(patch // slots == place, 0, slots)
    here = jnp.logical_and(new_owner[None, :] == me, new_slot[None, :] == slot)
    return jnp.broadcast_to(jnp.sum(jnp.where(here, code, 0), axis=1)[:, None, None], (CAP, 8, HALF))


def on_device(patches, new_owner, new_slot):
    slots = patches.shape[0]
    f32 = jnp.float32
    shape = jax.ShapeDtypeStruct
    block = shape((slots, FIELDS, EDGE, PLANE), f32)
    lines = shape((FIELDS, GHOST, EDGE, HALF), f32)
    side = shape((FIELDS, GHOST, GHOST, HALF), f32)

    def shift(value, axis, step):
        count = lax.axis_size(axis)
        return lax.ppermute(value, axis, [(i, (i + step) % count) for i in range(count)])

    x_low, x_high = shift(patches, "gx", 1), shift(patches, "gx", -1)
    prim, lines_z, lines_y, y_up, y_down, z_up, z_down = pl.pallas_call(
        pack_kernel,
        out_shape=[block, lines, lines, side, side, side, side],
        in_specs=[VMEM],
        out_specs=[VMEM] * 7,
        compiler_params=PARAMS,
        name="pack",
    )(patches)
    y_low, y_high = shift(y_up, "gy", 1), shift(y_down, "gy", -1)
    z_up, z_down, y_high = lax.optimization_barrier((z_up, z_down, y_high))
    z_low, z_high = shift(z_up, "gz", 1), shift(z_down, "gz", -1)
    change_x = pl.pallas_call(
        rows_kernel, out_shape=block, in_specs=[VMEM] * 3, out_specs=VMEM, compiler_params=PARAMS, name="rows"
    )(prim, x_low, x_high)
    change = pl.pallas_call(
        columns_kernel,
        out_shape=block,
        in_specs=[VMEM] * 4,
        out_specs=VMEM,
        scratch_shapes=[pltpu.VMEM(lines.shape, f32)],
        compiler_params=PARAMS,
        name="columns",
    )(change_x, lines_y, y_low, y_high)
    advanced = pl.pallas_call(
        finish_kernel,
        out_shape=block,
        in_specs=[VMEM] * 5,
        out_specs=VMEM,
        scratch_shapes=[pltpu.VMEM(lines.shape, f32)],
        compiler_params=PARAMS,
        name="finish",
    )(patches, change, lines_z, z_low, z_high)
    advanced, new_owner, new_slot = lax.optimization_barrier((advanced, new_owner, new_slot))
    members = lax.axis_size("gz")
    partner = lax.ppermute(advanced, "gz", [(i, i ^ 1) for i in range(members)])
    return pl.pallas_call(
        place_kernel,
        out_shape=shape((CAP, FIELDS, EDGE, PLANE), f32),
        in_specs=[VMEM] * 3,
        out_specs=ANY,
        scratch_shapes=[pltpu.VMEM((CAP, FIELDS, EDGE, PLANE), f32), pltpu.SemaphoreType.DMA((CAP,))],
        compiler_params=PARAMS,
        name="place",
    )(slot_codes(new_owner, new_slot, slots), advanced, partner)


def solution(mesh):
    in_specs = (P(("gx", "gy", "gz"), None, None, None), P(("gx", "gy")), P(("gx", "gy")))
    out_specs = P(("gx", "gy", "gz"), None, None, None)
    return jax.shard_map(
        on_device, mesh=mesh, in_specs=in_specs, out_specs=out_specs, check_vma=False
    )
```

```python
import jax
import jax.numpy as jnp
from jax import lax
from jax.experimental import pallas as pl
from jax.experimental.pallas import tpu as pltpu
from jax.sharding import PartitionSpec as P

EDGE = 16
GHOST = 4
CAP = 4
FIELDS = 6
PLANE = EDGE * EDGE
STRIP = GHOST * EDGE
HALF = 128

STEP_RATIO = 0.08
VMEM = pl.BlockSpec(memory_space=pltpu.VMEM)
ANY = pl.BlockSpec(memory_space=pl.ANY)
PARAMS = pltpu.CompilerParams(vmem_limit_bytes=6 * 1024 * 1024)


def to_primitive(u):
    density, mom_x, mom_y, mom_z, energy, species = u
    inverse = 1.0 / density
    vel_x, vel_y, vel_z = mom_x * inverse, mom_y * inverse, mom_z * inverse
    kinetic = 0.5 * (mom_x * vel_x + mom_y * vel_y + mom_z * vel_z)
    pressure = (2.0 / 3.0) * (energy - kinetic)
    return [density, vel_x, vel_y, vel_z, pressure, species * inverse]


def median_zero(second, third):
    return jnp.maximum(jnp.minimum(second, 0.0), jnp.minimum(jnp.maximum(second, 0.0), third))


def side_terms(state, normal):
    density, pressure = state[0], state[4]
    ratio = pressure / density
    speed = state[1 + normal]
    square = state[1] * state[1] + state[2] * state[2] + state[3] * state[3]
    specific = 1.5 * ratio + 0.5 * square
    signal = jnp.abs(speed) + jnp.sqrt((5.0 / 3.0) * ratio)
    return speed, specific, signal


def sweep(primitive, normal, at):
    plus, minus = [], []
    for value in primitive:
        after = at(value, 1)
        face = 37.0 * (value + after) - 8.0 * (at(value, -1) + at(value, 2)) + (at(value, -2) + at(value, 3))
        face = face * (1.0 / 60.0)
        face = jnp.minimum(jnp.maximum(face, jnp.minimum(value, after)), jnp.maximum(value, after))
        left_jump = value - at(face, -1)
        right_jump = face - value
        plus.append(value + median_zero(right_jump, 2.0 * left_jump))
        minus.append(at(value - median_zero(left_jump, 2.0 * right_jump), 1))
    left_speed, left_specific, left_signal = side_terms(plus, normal)
    right_speed, right_specific, right_signal = side_terms(minus, normal)
    signal = jnp.maximum(left_signal, right_signal)
    left_weight = 0.5 * plus[0] * (left_speed + signal)
    right_weight = 0.5 * minus[0] * (right_speed - signal)
    flux = [left_weight + right_weight]
    for k in (1, 2, 3):
        flux.append(left_weight * plus[k] + right_weight * minus[k])
    flux[1 + normal] = flux[1 + normal] + 0.5 * (plus[4] + minus[4])
    flux.append(
        left_weight * left_specific
        + right_weight * right_specific
        + 0.5 * (plus[4] * left_speed + minus[4] * right_speed)
    )
    flux.append(left_weight * plus[5] + right_weight * minus[5])
    return [f - at(f, -1) for f in flux]


def exchange_lanes(rows):
    source = lax.broadcasted_iota(jnp.int32, (PLANE, PLANE), 0)
    target = lax.broadcasted_iota(jnp.int32, (PLANE, PLANE), 1)
    wanted = ((target & (EDGE - 1)) << 4) | (target >> 4)
    swap = jnp.where(source == wanted, 1.0, 0.0).astype(jnp.bfloat16)
    parts = []
    for _ in range(3):
        parts.append(rows.astype(jnp.bfloat16))
        rows = rows - parts[-1].astype(jnp.float32)
    moved = jnp.dot(jnp.concatenate(parts, axis=0), swap, preferred_element_type=jnp.float32)
    count = rows.shape[0]
    return moved[:count] + moved[count : 2 * count] + moved[2 * count :]


def to_lines(first, second):
    left = lax.broadcasted_iota(jnp.int32, (2 * EDGE, HALF), 1) < STRIP
    rows = []
    for part in range(2):
        one = first.reshape(2 * EDGE, PLANE)[:, part * HALF : (part + 1) * HALF]
        two = second.reshape(2 * EDGE, PLANE)[:, part * HALF : (part + 1) * HALF]
        rows.append(jnp.where(left, one, pltpu.roll(two, STRIP, 1)))
        rows.append(jnp.where(left, pltpu.roll(one, STRIP, 1), two))
    lines = jnp.concatenate(rows, axis=0).T
    return lines[:STRIP], lines[STRIP:]


def from_lines(first, second):
    left = lax.broadcasted_iota(jnp.int32, (2 * EDGE, HALF), 1) < STRIP
    rows = jnp.concatenate([first, second], axis=0).T
    rows = [rows[k * 2 * EDGE : (k + 1) * 2 * EDGE] for k in range(4)]
    one, two = [], []
    for part in range(2):
        low, high = rows[2 * part], rows[2 * part + 1]
        one.append(jnp.where(left, low, pltpu.roll(high, STRIP, 1)))
        two.append(jnp.where(left, pltpu.roll(low, STRIP, 1), high))
    return jnp.concatenate(one, axis=1), jnp.concatenate(two, axis=1)


def pack_kernel(u_ref, prim_ref, lines_z, lines_y, y_up, y_down, z_up, z_down):
    slots = u_ref.shape[0]
    for p in range(slots):
        for q, value in enumerate(to_primitive([u_ref[p, q] for q in range(FIELDS)])):
            prim_ref[p, q] = value
    swapped = exchange_lanes(prim_ref[...].reshape(slots * FIELDS * EDGE, PLANE))
    swapped = swapped.reshape(slots, FIELDS, EDGE, PLANE)
    for pair in range(0, FIELDS, 2):
        for ref, pieces in (
            (lines_z, to_lines(prim_ref[:, pair], prim_ref[:, pair + 1])),
            (lines_y, to_lines(swapped[:, pair], swapped[:, pair + 1])),
        ):
            for k in range(2):
                ref[pair + k] = pieces[k].reshape(GHOST, EDGE, HALF)
    for ref, up, down in ((lines_z, z_up, z_down), (lines_y, y_up, y_down)):
        up[...] = ref[:, :, EDGE - GHOST :, :]
        down[...] = ref[:, :, :GHOST, :]


def row_at(value, k):
    height = value.shape[0]
    return pltpu.roll(value, (-k) % height, 0)


def sweep_lines(low, lines, high, normal, change):
    for group in range(GHOST):
        extended = [
            jnp.concatenate([low[q, group], lines[q, group], high[q, group]], axis=0) for q in range(FIELDS)
        ]
        for q, value in enumerate(sweep(extended, normal, row_at)):
            change[q, group] = value[GHOST : GHOST + EDGE]


def rows_kernel(prim_ref, low_ref, high_ref, out_ref):
    slots = out_ref.shape[0]
    for half in range(2):
        lanes = slice(half * HALF, half * HALF + HALF)
        low = to_primitive([low_ref[slots - 1, q, EDGE - GHOST :, lanes] for q in range(FIELDS)])
        high = to_primitive([high_ref[0, q, :GHOST, lanes] for q in range(FIELDS)])
        lines = [
            jnp.concatenate([low[q]] + [prim_ref[p, q, :, lanes] for p in range(slots)] + [high[q]], axis=0)
            for q in range(FIELDS)
        ]
        for q, value in enumerate(sweep(lines, 0, row_at)):
            for p in range(slots):
                first = GHOST + p * EDGE
                out_ref[p, q, :, lanes] = value[first : first + EDGE]


def columns_kernel(before_ref, lines_y, y_low, y_high, out_ref, change_y):
    slots = out_ref.shape[0]
    sweep_lines(y_low, lines_y, y_high, 1, change_y)
    for pair in range(0, FIELDS, 2):
        parts = from_lines(change_y[pair].reshape(STRIP, HALF), change_y[pair + 1].reshape(STRIP, HALF))
        for k in range(2):
            out_ref[:, pair + k] = parts[k].reshape(slots, EDGE, PLANE)
    flat = exchange_lanes(out_ref[...].reshape(slots * FIELDS * EDGE, PLANE))
    out_ref[...] = flat.reshape(slots, FIELDS, EDGE, PLANE) + before_ref[...]


def finish_kernel(u_ref, change_ref, lines_z, z_low, z_high, out_ref, change_z):
    slots = u_ref.shape[0]
    sweep_lines(z_low, lines_z, z_high, 2, change_z)
    for pair in range(0, FIELDS, 2):
        parts = from_lines(change_z[pair].reshape(STRIP, HALF), change_z[pair + 1].reshape(STRIP, HALF))
        for k in range(2):
            total = change_ref[:, pair + k] + parts[k].reshape(slots, EDGE, PLANE)
            out_ref[:, pair + k] = u_ref[:, pair + k] - STEP_RATIO * total


def place_kernel(code_ref, own_ref, partner_ref, out_ref, held, sems):
    slots = own_ref.shape[0]
    copies = []
    for s in range(CAP):
        code = jnp.concatenate([code_ref[s]] * 2, axis=1)
        for q in range(FIELDS):
            for half in range(2):
                rows = slice(half * 8, half * 8 + 8)
                value = jnp.zeros((8, PLANE), jnp.float32)
                for p in range(slots):
                    value = jnp.where(code == 1 + p, own_ref[p, q, rows, :], value)
                    value = jnp.where(code == 1 + slots + p, partner_ref[p, q, rows, :], value)
                held[s, q, rows, :] = value
        copies.append(pltpu.make_async_copy(held.at[s], out_ref.at[s], sems.at[s]))
        copies[s].start()
    for copy in copies:
        copy.wait()


def slot_codes(new_owner, new_slot, slots):
    members = lax.axis_size("gz")
    place = lax.axis_index("gz")
    me = (lax.axis_index("gx") * lax.axis_size("gy") + lax.axis_index("gy")) * members + place
    patch = lax.broadcasted_iota(jnp.int32, (CAP, members * slots), 1)
    slot = lax.broadcasted_iota(jnp.int32, (CAP, members * slots), 0)
    code = patch % slots + 1 + jnp.where(patch // slots == place, 0, slots)
    here = jnp.logical_and(new_owner[None, :] == me, new_slot[None, :] == slot)
    return jnp.broadcast_to(jnp.sum(jnp.where(here, code, 0), axis=1)[:, None, None], (CAP, 8, HALF))


def on_device(patches, new_owner, new_slot):
    slots = patches.shape[0]
    f32 = jnp.float32
    shape = jax.ShapeDtypeStruct
    block = shape((slots, FIELDS, EDGE, PLANE), f32)
    lines = shape((FIELDS, GHOST, EDGE, HALF), f32)
    side = shape((FIELDS, GHOST, GHOST, HALF), f32)

    def shift(value, axis, step):
        count = lax.axis_size(axis)
        return lax.ppermute(value, axis, [(i, (i + step) % count) for i in range(count)])

    x_high, x_low = shift(patches, "gx", -1), shift(patches, "gx", 1)
    prim, lines_z, lines_y, y_up, y_down, z_up, z_down = pl.pallas_call(
        pack_kernel,
        out_shape=[block, lines, lines, side, side, side, side],
        in_specs=[VMEM],
        out_specs=[VMEM] * 7,
        compiler_params=PARAMS,
        name="pack",
    )(patches)
    y_low, y_high = shift(y_up, "gy", 1), shift(y_down, "gy", -1)
    z_up, z_down, y_high = lax.optimization_barrier((z_up, z_down, y_high))
    z_low, z_high = shift(z_up, "gz", 1), shift(z_down, "gz", -1)
    change_x = pl.pallas_call(
        rows_kernel, out_shape=block, in_specs=[VMEM] * 3, out_specs=VMEM, compiler_params=PARAMS, name="rows"
    )(prim, x_low, x_high)
    change = pl.pallas_call(
        columns_kernel,
        out_shape=block,
        in_specs=[VMEM] * 4,
        out_specs=VMEM,
        scratch_shapes=[pltpu.VMEM(lines.shape, f32)],
        compiler_params=PARAMS,
        name="columns",
    )(change_x, lines_y, y_low, y_high)
    advanced = pl.pallas_call(
        finish_kernel,
        out_shape=block,
        in_specs=[VMEM] * 5,
        out_specs=VMEM,
        scratch_shapes=[pltpu.VMEM(lines.shape, f32)],
        compiler_params=PARAMS,
        name="finish",
    )(patches, change, lines_z, z_low, z_high)
    advanced, new_owner, new_slot = lax.optimization_barrier((advanced, new_owner, new_slot))
    members = lax.axis_size("gz")
    partner = lax.ppermute(advanced, "gz", [(i, i ^ 1) for i in range(members)])
    return pl.pallas_call(
        place_kernel,
        out_shape=shape((CAP, FIELDS, EDGE, PLANE), f32),
        in_specs=[VMEM] * 3,
        out_specs=ANY,
        scratch_shapes=[pltpu.VMEM((CAP, FIELDS, EDGE, PLANE), f32), pltpu.SemaphoreType.DMA((CAP,))],
        compiler_params=PARAMS,
        name="place",
    )(slot_codes(new_owner, new_slot, slots), advanced, partner)


def solution(mesh):
    in_specs = (P(("gx", "gy", "gz"), None, None, None), P(("gx", "gy")), P(("gx", "gy")))
    out_specs = P(("gx", "gy", "gz"), None, None, None)
    return jax.shard_map(
        on_device, mesh=mesh, in_specs=in_specs, out_specs=out_specs, check_vma=False
    )
```

```python
import jax
import jax.numpy as jnp
from jax import lax
from jax.experimental import pallas as pl
from jax.experimental.pallas import tpu as pltpu
from jax.sharding import PartitionSpec as P

EDGE = 16
GHOST = 4
CAP = 4
FIELDS = 6
PLANE = EDGE * EDGE
STRIP = GHOST * EDGE
HALF = 128

STEP_RATIO = 0.08
VMEM = pl.BlockSpec(memory_space=pltpu.VMEM)
ANY = pl.BlockSpec(memory_space=pl.ANY)
HELD = pltpu.VMEM((FIELDS, 2 * EDGE + 3 * 8, HALF), jnp.float32)
PARAMS = pltpu.CompilerParams(vmem_limit_bytes=6 * 1024 * 1024)


def to_primitive(u):
    density, mom_x, mom_y, mom_z, energy, species = u
    inverse = 1.0 / density
    vel_x, vel_y, vel_z = mom_x * inverse, mom_y * inverse, mom_z * inverse
    kinetic = 0.5 * (mom_x * vel_x + mom_y * vel_y + mom_z * vel_z)
    pressure = (2.0 / 3.0) * (energy - kinetic)
    return [density, vel_x, vel_y, vel_z, pressure, species * inverse]


def median_zero(second, third):
    return jnp.maximum(jnp.minimum(second, 0.0), jnp.minimum(jnp.maximum(second, 0.0), third))


def side_terms(state, normal):
    density, pressure = state[0], state[4]
    ratio = pressure / density
    speed = state[1 + normal]
    square = state[1] * state[1] + state[2] * state[2] + state[3] * state[3]
    specific = 1.5 * ratio + 0.5 * square
    signal = jnp.abs(speed) + jnp.sqrt((5.0 / 3.0) * ratio)
    return speed, specific, signal


def sweep(primitive, normal, at, held):
    plus, minus = [], []
    for q, value in enumerate(primitive):
        count = value.shape[0]
        held[q, 8 : 8 + count, :] = value
        before2, before, after, after2, after3 = [held[q, 8 + k : 8 + k + count, :] for k in (-2, -1, 1, 2, 3)]
        face = 37.0 * (value + after) - 8.0 * (before + after2) + (before2 + after3)
        face = face * (1.0 / 60.0)
        face = jnp.minimum(jnp.maximum(face, jnp.minimum(value, after)), jnp.maximum(value, after))
        left_jump = value - at(face, -1)
        right_jump = face - value
        plus.append(value + median_zero(right_jump, 2.0 * left_jump))
        minus.append(at(value - median_zero(left_jump, 2.0 * right_jump), 1))
    left_speed, left_specific, left_signal = side_terms(plus, normal)
    right_speed, right_specific, right_signal = side_terms(minus, normal)
    signal = jnp.maximum(left_signal, right_signal)
    left_weight = 0.5 * plus[0] * (left_speed + signal)
    right_weight = 0.5 * minus[0] * (right_speed - signal)
    flux = [left_weight + right_weight]
    for k in (1, 2, 3):
        flux.append(left_weight * plus[k] + right_weight * minus[k])
    flux[1 + normal] = flux[1 + normal] + 0.5 * (plus[4] + minus[4])
    flux.append(
        left_weight * left_specific
        + right_weight * right_specific
        + 0.5 * (plus[4] * left_speed + minus[4] * right_speed)
    )
    flux.append(left_weight * plus[5] + right_weight * minus[5])
    return [f - at(f, -1) for f in flux]


def exchange_lanes(rows):
    source = lax.broadcasted_iota(jnp.int32, (PLANE, PLANE), 0)
    target = lax.broadcasted_iota(jnp.int32, (PLANE, PLANE), 1)
    wanted = ((target & (EDGE - 1)) << 4) | (target >> 4)
    swap = jnp.where(source == wanted, 1.0, 0.0).astype(jnp.bfloat16)
    parts = []
    for _ in range(3):
        parts.append(rows.astype(jnp.bfloat16))
        rows = rows - parts[-1].astype(jnp.float32)
    moved = jnp.dot(jnp.concatenate(parts, axis=0), swap, preferred_element_type=jnp.float32)
    count = rows.shape[0]
    return moved[:count] + moved[count : 2 * count] + moved[2 * count :]


def to_lines(first, second):
    left = lax.broadcasted_iota(jnp.int32, (2 * EDGE, HALF), 1) < STRIP
    rows = []
    for part in range(2):
        one = first.reshape(2 * EDGE, PLANE)[:, part * HALF : (part + 1) * HALF]
        two = second.reshape(2 * EDGE, PLANE)[:, part * HALF : (part + 1) * HALF]
        rows.append(jnp.where(left, one, pltpu.roll(two, STRIP, 1)))
        rows.append(jnp.where(left, pltpu.roll(one, STRIP, 1), two))
    lines = jnp.concatenate(rows, axis=0).T
    return lines[:STRIP], lines[STRIP:]


def from_lines(first, second):
    left = lax.broadcasted_iota(jnp.int32, (2 * EDGE, HALF), 1) < STRIP
    rows = jnp.concatenate([first, second], axis=0).T
    rows = [rows[k * 2 * EDGE : (k + 1) * 2 * EDGE] for k in range(4)]
    one, two = [], []
    for part in range(2):
        low, high = rows[2 * part], rows[2 * part + 1]
        one.append(jnp.where(left, low, pltpu.roll(high, STRIP, 1)))
        two.append(jnp.where(left, pltpu.roll(low, STRIP, 1), high))
    return jnp.concatenate(one, axis=1), jnp.concatenate(two, axis=1)


def pack_kernel(u_ref, prim_ref, lines_z, lines_y, y_up, y_down, z_up, z_down):
    slots = u_ref.shape[0]
    for p in range(slots):
        for q, value in enumerate(to_primitive([u_ref[p, q] for q in range(FIELDS)])):
            prim_ref[p, q] = value
    swapped = exchange_lanes(prim_ref[...].reshape(slots * FIELDS * EDGE, PLANE))
    swapped = swapped.reshape(slots, FIELDS, EDGE, PLANE)
    for pair in range(0, FIELDS, 2):
        for ref, pieces in (
            (lines_z, to_lines(prim_ref[:, pair], prim_ref[:, pair + 1])),
            (lines_y, to_lines(swapped[:, pair], swapped[:, pair + 1])),
        ):
            for k in range(2):
                ref[pair + k] = pieces[k].reshape(GHOST, EDGE, HALF)
    for ref, up, down in ((lines_z, z_up, z_down), (lines_y, y_up, y_down)):
        up[...] = ref[:, :, EDGE - GHOST :, :]
        down[...] = ref[:, :, :GHOST, :]


def row_at(value, k):
    height = value.shape[0]
    return pltpu.roll(value, (-k) % height, 0)


def sweep_lines(low, lines, high, normal, change, held):
    for group in range(GHOST):
        extended = [
            jnp.concatenate([low[q, group], lines[q, group], high[q, group]], axis=0) for q in range(FIELDS)
        ]
        for q, value in enumerate(sweep(extended, normal, row_at, held)):
            change[q, group] = value[GHOST : GHOST + EDGE]


def rows_kernel(prim_ref, low_ref, high_ref, out_ref, held):
    slots = out_ref.shape[0]
    for half in range(2):
        lanes = slice(half * HALF, half * HALF + HALF)
        low = to_primitive([low_ref[slots - 1, q, EDGE - GHOST :, lanes] for q in range(FIELDS)])
        high = to_primitive([high_ref[0, q, :GHOST, lanes] for q in range(FIELDS)])
        lines = [
            jnp.concatenate([low[q]] + [prim_ref[p, q, :, lanes] for p in range(slots)] + [high[q]], axis=0)
            for q in range(FIELDS)
        ]
        for q, value in enumerate(sweep(lines, 0, row_at, held)):
            for p in range(slots):
                first = GHOST + p * EDGE
                out_ref[p, q, :, lanes] = value[first : first + EDGE]


def columns_kernel(before_ref, lines_y, y_low, y_high, out_ref, change_y, held):
    slots = out_ref.shape[0]
    sweep_lines(y_low, lines_y, y_high, 1, change_y, held)
    for pair in range(0, FIELDS, 2):
        parts = from_lines(change_y[pair].reshape(STRIP, HALF), change_y[pair + 1].reshape(STRIP, HALF))
        for k in range(2):
            out_ref[:, pair + k] = parts[k].reshape(slots, EDGE, PLANE)
    flat = exchange_lanes(out_ref[...].reshape(slots * FIELDS * EDGE, PLANE))
    out_ref[...] = flat.reshape(slots, FIELDS, EDGE, PLANE) + before_ref[...]


def finish_kernel(u_ref, change_ref, lines_z, z_low, z_high, out_ref, change_z, held):
    slots = u_ref.shape[0]
    sweep_lines(z_low, lines_z, z_high, 2, change_z, held)
    for pair in range(0, FIELDS, 2):
        parts = from_lines(change_z[pair].reshape(STRIP, HALF), change_z[pair + 1].reshape(STRIP, HALF))
        for k in range(2):
            total = change_ref[:, pair + k] + parts[k].reshape(slots, EDGE, PLANE)
            out_ref[:, pair + k] = u_ref[:, pair + k] - STEP_RATIO * total


def place_kernel(code_ref, own_ref, partner_ref, out_ref, held, sems):
    slots = own_ref.shape[0]
    copies = []
    for s in range(CAP):
        code = jnp.concatenate([code_ref[s]] * 2, axis=1)
        for q in range(FIELDS):
            for half in range(2):
                rows = slice(half * 8, half * 8 + 8)
                value = jnp.zeros((8, PLANE), jnp.float32)
                for p in range(slots):
                    value = jnp.where(code == 1 + p, own_ref[p, q, rows, :], value)
                    value = jnp.where(code == 1 + slots + p, partner_ref[p, q, rows, :], value)
                held[s, q, rows, :] = value
        copies.append(pltpu.make_async_copy(held.at[s], out_ref.at[s], sems.at[s]))
        copies[s].start()
    for copy in copies:
        copy.wait()


def slot_codes(new_owner, new_slot, slots):
    members = lax.axis_size("gz")
    place = lax.axis_index("gz")
    me = (lax.axis_index("gx") * lax.axis_size("gy") + lax.axis_index("gy")) * members + place
    patch = lax.broadcasted_iota(jnp.int32, (CAP, members * slots), 1)
    slot = lax.broadcasted_iota(jnp.int32, (CAP, members * slots), 0)
    code = patch % slots + 1 + jnp.where(patch // slots == place, 0, slots)
    here = jnp.logical_and(new_owner[None, :] == me, new_slot[None, :] == slot)
    return jnp.broadcast_to(jnp.sum(jnp.where(here, code, 0), axis=1)[:, None, None], (CAP, 8, HALF))


def on_device(patches, new_owner, new_slot):
    slots = patches.shape[0]
    f32 = jnp.float32
    shape = jax.ShapeDtypeStruct
    block = shape((slots, FIELDS, EDGE, PLANE), f32)
    lines = shape((FIELDS, GHOST, EDGE, HALF), f32)
    side = shape((FIELDS, GHOST, GHOST, HALF), f32)

    def shift(value, axis, step):
        count = lax.axis_size(axis)
        return lax.ppermute(value, axis, [(i, (i + step) % count) for i in range(count)])

    x_high, x_low = shift(patches, "gx", -1), shift(patches, "gx", 1)
    prim, lines_z, lines_y, y_up, y_down, z_up, z_down = pl.pallas_call(
        pack_kernel,
        out_shape=[block, lines, lines, side, side, side, side],
        in_specs=[VMEM],
        out_specs=[VMEM] * 7,
        compiler_params=PARAMS,
        name="pack",
    )(patches)
    y_low, y_high = shift(y_up, "gy", 1), shift(y_down, "gy", -1)
    z_up, z_down, y_high = lax.optimization_barrier((z_up, z_down, y_high))
    z_low, z_high = shift(z_up, "gz", 1), shift(z_down, "gz", -1)
    change_x = pl.pallas_call(
        rows_kernel, out_shape=block, in_specs=[VMEM] * 3, out_specs=VMEM, scratch_shapes=[HELD], compiler_params=PARAMS, name="rows"
    )(prim, x_low, x_high)
    change = pl.pallas_call(
        columns_kernel,
        out_shape=block,
        in_specs=[VMEM] * 4,
        out_specs=VMEM,
        scratch_shapes=[pltpu.VMEM(lines.shape, f32), HELD],
        compiler_params=PARAMS,
        name="columns",
    )(change_x, lines_y, y_low, y_high)
    advanced = pl.pallas_call(
        finish_kernel,
        out_shape=block,
        in_specs=[VMEM] * 5,
        out_specs=VMEM,
        scratch_shapes=[pltpu.VMEM(lines.shape, f32), HELD],
        compiler_params=PARAMS,
        name="finish",
    )(patches, change, lines_z, z_low, z_high)
    advanced, new_owner, new_slot = lax.optimization_barrier((advanced, new_owner, new_slot))
    members = lax.axis_size("gz")
    partner = lax.ppermute(advanced, "gz", [(i, i ^ 1) for i in range(members)])
    return pl.pallas_call(
        place_kernel,
        out_shape=shape((CAP, FIELDS, EDGE, PLANE), f32),
        in_specs=[VMEM] * 3,
        out_specs=ANY,
        scratch_shapes=[pltpu.VMEM((CAP, FIELDS, EDGE, PLANE), f32), pltpu.SemaphoreType.DMA((CAP,))],
        compiler_params=PARAMS,
        name="place",
    )(slot_codes(new_owner, new_slot, slots), advanced, partner)


def solution(mesh):
    in_specs = (P(("gx", "gy", "gz"), None, None, None), P(("gx", "gy")), P(("gx", "gy")))
    out_specs = P(("gx", "gy", "gz"), None, None, None)
    return jax.shard_map(
        on_device, mesh=mesh, in_specs=in_specs, out_specs=out_specs, check_vma=False
    )
```
